128 devices in a mesh: ctx: 32 (over z, y_lo, x), head: 4 (over y_hi, core).
Axes of the slice: x: 4, y: 4 (y_hi: 2, y_lo: 2; y = y_hi * 2 + y_lo), z: 4, core: 2. Of those that a mesh axis runs over, the one named last changes fastest.
Arguments:
- queries: bfloat16 [16384, 2560], P('ctx', 'head'), may hold values from -6 to 6, as said below
- keys: bfloat16 [16384, 512], P('ctx', 'head'), may hold values from -6 to 6, as said below
- values: bfloat16 [16384, 512], P('ctx', 'head'), may hold values from -6 to 6
- lengths: int32 [32], replicated, may hold values from 1 to 1024, 16384 in all
- w_out: bfloat16 [5120, 2560], P(None, 'head'), may hold values from -0.125 to 0.125
- grad_y: bfloat16 [16384, 5120], P(('ctx', 'head')), may hold values from -6 to 6
Outputs:
- projected: bfloat16 [16384, 5120], P(('ctx', 'head'))
- grad_queries: bfloat16 [16384, 2560], P('ctx', 'head')
- grad_keys: bfloat16 [16384, 512], P('ctx', 'head')
- grad_values: bfloat16 [16384, 512], P('ctx', 'head')
- grad_weight: float32 [5120, 2560], P('ctx', 'head')
The draws below stay inside these ranges and needn't reach their ends.
Inputs may be any that keep to these rules, and one draw needn't show every extreme that they name: `queries`: queries as drawn. `keys`: keys as drawn. The lengths sum to 16384; the longest is exactly 1024.
All inputs are finite; a program needn't handle non-finite values.
Results may differ from the reference program's by a relative error of at most 0.025.
Values may be sent and summed in bfloat16 or wider, within the bound.
A program may use at most 128 MiB of HBM per device.

```python
import math
import jax
import jax.numpy as jnp
import numpy as np
from jax import lax

D = 5120
HEADS = 20
KV_HEADS = 4
E = 128
WINDOW = 2
TOK_DEV = 512
TOKENS = 16384
DOC_MOST = 1024
DOCS = 32


def paired_draw(key, lift):
    base_q, base_k, signs, q_lift, k_lift, gap_key = jax.random.split(key, 6)
    group_ratio = HEADS // KV_HEADS
    positions = jnp.arange(TOKENS, dtype=jnp.int32)
    chosen = positions % 61 == 7
    before = positions % 61 == 6
    normal_q = jax.random.truncated_normal(base_q, -4.0, 4.0, (TOKENS, KV_HEADS, group_ratio, E))
    normal_k = jax.random.truncated_normal(base_k, -4.0, 4.0, (TOKENS, KV_HEADS, E))
    drawn_q = normal_q
    drawn_k = normal_k
    direction = jnp.where(jax.random.bernoulli(signs, 0.5, (TOKENS, KV_HEADS, E)), 1.0, -1.0)
    strength_q = jax.random.uniform(q_lift, (TOKENS, KV_HEADS, group_ratio, 1), minval=3.0, maxval=5.5)
    strength_k = jax.random.uniform(k_lift, (TOKENS, KV_HEADS, 1), minval=3.0, maxval=5.5)
    offset = jax.random.uniform(gap_key, (TOKENS, KV_HEADS, 1), minval=1.8, maxval=3.0)
    root = math.sqrt(E)
    query_peak = strength_q * direction[:, :, None, :]
    key_peak = strength_k * direction
    next_direction = jnp.roll(direction, -1, axis=0)
    next_strength = jnp.roll(strength_k, -1, axis=0)
    next_offset = jnp.roll(offset, -1, axis=0)
    key_near = (next_strength - next_offset / (5.5 * root)) * next_direction
    active = lift > 0.5
    queries_out = jnp.where(chosen[:, None, None, None] & active, query_peak, drawn_q)
    keys_out = jnp.where(chosen[:, None, None] & active, key_peak, drawn_k)
    keys_out = jnp.where(before[:, None, None] & active, key_near, keys_out)
    return (queries_out.reshape(TOKENS, HEADS * E), keys_out.reshape(TOKENS, KV_HEADS * E))


def draw_queries(key, part):
    lift = 0.0
    return paired_draw(key, lift)[0].astype(jnp.bfloat16)


def draw_keys(key, part):
    lift = 0.0
    return paired_draw(key, lift)[1].astype(jnp.bfloat16)


def levels(key, dims, pieces, smallest, top_value):
    def one(position, blocks):
        steps = jax.random.uniform(jax.random.fold_in(jax.random.fold_in(key, 6), position), (blocks,), jnp.float32, smallest / len(pieces), top_value / len(pieces))
        return jnp.repeat(jnp.exp(steps), dims[position] // blocks).reshape((-1,) + (1,) * (len(dims) - position - 1))

    level = one(*pieces[0])
    for cut in pieces[1:]:
        level = level * one(*cut)
    return level


def profile(amount, total, bound, lean):
    weights = [(1 << 20) // math.isqrt(grade ** lean) + 1 for grade in range(2, amount + 1)]
    spare, given = total - bound - (amount - 1), [1] * (amount - 1)
    while spare > 0:
        candidates = [i for i in range(amount - 1) if given[i] < bound]
        mass, budget = sum([weights[i] for i in candidates]), spare
        for i in candidates:
            extra = min(bound - given[i], max(1, budget * weights[i] // mass), spare)
            given[i] = given[i] + extra
            spare = spare - extra
    return np.array([bound] + given)


def uneven_parts(own_key, count, total, most, slope):
    if count == 2:
        one = jax.random.randint(own_key, (), max(1, total - most), min(most, total - 1) + 1)
        return jnp.stack([one, total - one])
    sizes = jnp.asarray(profile(count, total, most, slope), jnp.int32)
    pairs = (count - 1) // 2
    donor, taker = sizes[1:1 + 2 * pairs:2], sizes[2:2 + 2 * pairs:2]
    margin = jnp.minimum(donor - 1, most - taker)
    passed = jax.random.randint(jax.random.fold_in(own_key, 1), (pairs,), 0, 1 << 20) % (margin + 1)
    sizes = sizes.at[1:1 + 2 * pairs:2].set(donor - passed).at[2:2 + 2 * pairs:2].set(taker + passed)
    return sizes[jax.random.permutation(jax.random.fold_in(own_key, 2), count)]


def centred(rng, extent, spread, bound, shards=(), kind=jnp.bfloat16):
    entries = spread * jax.random.normal(rng, extent, jnp.float32)
    if shards:
        entries = entries * levels(rng, extent, shards, -0.22, 0.18)
    return jnp.clip(entries, -bound, bound).astype(kind)


def setup_inputs(seed: int = 0) -> dict:
    splits = jax.random.split(jax.random.key(seed), 7)
    return {
        "queries": draw_queries(jax.random.fold_in(splits[6], 71), 0),
        "keys": draw_keys(jax.random.fold_in(splits[6], 71), 0),
        "values": centred(splits[2], (TOKENS, KV_HEADS * E), 1.0, 6.0, ((0, 32), (1, 4))),
        "lengths": uneven_parts(splits[3], DOCS, TOKENS, DOC_MOST, 2).astype(jnp.int32),
        "w_out": centred(splits[4], (D, HEADS * E), (HEADS * E) ** -0.5, 0.125, ((1, 4),)),
        "grad_y": centred(splits[5], (TOKENS, D), 1.0, 6.0, ((0, 128),)),
    }


masked_score = -1e30


def document_index(positions, doc_ends):
    return jnp.sum((positions[:, None] >= doc_ends[None, :]).astype(jnp.int32), axis=1)


def visibility(query_pos, key_pos, doc_ends):
    same_doc = document_index(query_pos, doc_ends)[:, None] == document_index(key_pos, doc_ends)[None, :]
    causal = key_pos[None, :] <= query_pos[:, None]
    return same_doc & causal & (key_pos[None, :] >= 0)


def reference(queries, keys, values, lengths, w_out, grad_y):
    score_scale = E ** -0.5
    group_ratio = HEADS // KV_HEADS
    reach = WINDOW * TOK_DEV
    width_keys = reach + TOK_DEV
    doc_ends = jnp.cumsum(lengths).astype(jnp.int32)
    upstream = jnp.dot(grad_y, w_out, preferred_element_type=jnp.float32).astype(jnp.bfloat16)
    front = jnp.zeros((reach, KV_HEADS * E), jnp.bfloat16)
    padded_keys = jnp.concatenate([front, keys], axis=0)
    padded_values = jnp.concatenate([front, values], axis=0)
    offsets = jnp.arange(TOK_DEV, dtype=jnp.int32)
    key_offsets = jnp.arange(width_keys, dtype=jnp.int32)

    def one_block(grads, block_index):
        grad_k, grad_v = grads
        first_row = (block_index * TOK_DEV).astype(jnp.int32)
        query_tiles = lax.dynamic_slice_in_dim(queries, first_row, TOK_DEV, 0)
        query_tiles = query_tiles.reshape(TOK_DEV, KV_HEADS, group_ratio, E).astype(jnp.float32)
        upstream_tiles = lax.dynamic_slice_in_dim(upstream, first_row, TOK_DEV, 0)
        upstream_tiles = upstream_tiles.reshape(TOK_DEV, KV_HEADS, group_ratio, E).astype(jnp.float32)
        key_tiles = lax.dynamic_slice_in_dim(padded_keys, first_row, width_keys, 0)
        key_tiles = key_tiles.reshape(width_keys, KV_HEADS, E).astype(jnp.float32)
        value_tiles = lax.dynamic_slice_in_dim(padded_values, first_row, width_keys, 0)
        value_tiles = value_tiles.reshape(width_keys, KV_HEADS, E).astype(jnp.float32)
        mask = visibility(first_row + offsets, first_row - reach + key_offsets, doc_ends)
        scores = jnp.einsum("tgre,kge->grtk", query_tiles, key_tiles) * score_scale
        scores = jnp.where(mask, scores, masked_score)
        row_max = jnp.max(scores, axis=-1, keepdims=True)
        row_total = jnp.sum(jnp.where(mask, jnp.exp(scores - row_max), 0.0), axis=-1, keepdims=True)
        log_total = row_max + jnp.log(row_total)
        weights_low = jnp.where(mask, jnp.exp(scores - log_total), 0.0).astype(jnp.bfloat16)
        weights = lax.optimization_barrier(weights_low).astype(jnp.float32)
        attended = jnp.einsum("grtk,kge->tgre", weights, value_tiles).astype(jnp.bfloat16)
        attended_wide = lax.optimization_barrier(attended).astype(jnp.float32)
        row_delta = jnp.sum(upstream_tiles * attended_wide, axis=-1).transpose(1, 2, 0)
        grad_prob = jnp.einsum("tgre,kge->grtk", upstream_tiles, value_tiles)
        score_low = (weights * (grad_prob - row_delta[..., None])).astype(jnp.bfloat16)
        grad_score = lax.optimization_barrier(score_low).astype(jnp.float32)
        grad_query = (jnp.einsum("grtk,kge->tgre", grad_score, key_tiles) * score_scale).astype(jnp.bfloat16)
        key_part = jnp.einsum("grtk,tgre->kge", grad_score, query_tiles) * score_scale
        value_part = jnp.einsum("grtk,tgre->kge", weights, upstream_tiles)
        old_k = lax.dynamic_slice_in_dim(grad_k, first_row, width_keys, 0)
        grad_k = lax.dynamic_update_slice_in_dim(grad_k, old_k + key_part.reshape(width_keys, KV_HEADS * E), first_row, 0)
        old_v = lax.dynamic_slice_in_dim(grad_v, first_row, width_keys, 0)
        grad_v = lax.dynamic_update_slice_in_dim(grad_v, old_v + value_part.reshape(width_keys, KV_HEADS * E), first_row, 0)
        return (grad_k, grad_v), (attended.reshape(TOK_DEV, HEADS * E), grad_query.reshape(TOK_DEV, HEADS * E))

    empty = jnp.zeros((TOKENS + reach, KV_HEADS * E), jnp.float32)
    (grad_k, grad_v), (attended, grad_queries) = lax.scan(one_block, (empty, empty), jnp.arange(TOKENS // TOK_DEV, dtype=jnp.int32))
    attended = attended.reshape(TOKENS, HEADS * E)
    grad_queries = grad_queries.reshape(TOKENS, HEADS * E)
    projected = jnp.dot(attended, w_out.T, preferred_element_type=jnp.float32).astype(jnp.bfloat16)
    grad_weight = jnp.dot(grad_y.T, attended, preferred_element_type=jnp.float32) * (TOKENS ** -0.5)
    grad_keys = grad_k[reach:].astype(jnp.bfloat16)
    grad_values = grad_v[reach:].astype(jnp.bfloat16)
    return (projected, grad_queries, grad_keys, grad_values, grad_weight)
```

```python
import functools
import math

import jax
import jax.numpy as jnp
from jax import lax
from jax.experimental import pallas as pl
from jax.experimental.pallas import tpu as pltpu
from jax.sharding import PartitionSpec as P

E = 128
MESH = pl.DeviceIdType.MESH
F32 = jnp.float32
BF16 = jnp.bfloat16
NT = (((1,), (1,)), ((), ()))
TN = (((0,), (0,)), ((), ()))
NN = (((1,), (0,)), ((), ()))
RATIO = 5
ROWS = 512
COLS = RATIO * E
WIDTH = 9 * E
MODEL = 5120
GROUP = 640
PIECE = 160
MASKED = -1e30
Z_STEPS = (2, 1, 3, 0)


def dot(a, b, dims):
    return lax.dot_general(a, b, dims, preferred_element_type=F32)


def stack_heads(ref, first):
    return jnp.concatenate(
        [ref[pl.ds(first, E), r * E : (r + 1) * E] for r in range(RATIO)], axis=0
    )


def kernel(
    q_hbm,
    k_hbm,
    v_hbm,
    lengths,
    w_hbm,
    gy_hbm,
    proj_out,
    dq_out,
    dk_out,
    dv_out,
    gw_out,
    q,
    kw,
    vw,
    w,
    cot,
    att,
    up,
    up_acc,
    probs,
    scores,
    dk_acc,
    dv_acc,
    home_send,
    home_recv,
    part,
    core_recv,
    y_send,
    y_recv,
    stage,
    ax_recv,
    az_send,
    az_recv,
    bz_recv,
    bx_send,
    bx_recv,
    l_send,
    l_recv,
    local_sem,
    kv_ss,
    kv_rs,
    own_ss,
    own_rs,
    ag_ss,
    ag_rs,
    fw_ss,
    fw_rs,
    home_ss,
    home_rs,
    pc_ss,
    pc_rs,
    py_ss,
    py_rs,
    ax_ss,
    ax_rs,
    az_ss,
    az_rs,
    bz_ss,
    bz_rs,
    bx_ss,
    bx_rs,
    l_ss,
    l_rs,
):
    c = lax.axis_index("ctx")
    h = lax.axis_index("head")
    z, yl, x = c // 8, (c // 4) % 2, c % 4
    core, yh = h % 2, h // 2
    h_core = h + 1 - 2 * core
    h_far = (h + 2) % 4
    core_dev = (c, h_core)
    far_dev = (c, h_far)
    lo_dev = (c + 4 - 8 * yl, h)

    def x_dev(step):
        return (c - x + (x + step) % 4, h)

    def z_dev(step):
        return ((c + 8 * step) % 32, h)

    def c_dev(step):
        return ((c + step + 32) % 32, h)

    sends = []

    def send(src, dst, ss, rs, device):
        copy = pltpu.make_async_remote_copy(
            src_ref=src, dst_ref=dst, send_sem=ss, recv_sem=rs, device_id=device, device_id_type=MESH
        )
        copy.start()
        sends.append(copy)
        return copy

    def rows_of(head):
        return pl.ds(pl.multiple_of(head * 128, 128), 128)

    own_rows = rows_of(h)
    far_rows = rows_of(h_far)

    def group_cols(n):
        first = (((z + Z_STEPS[n // 2]) % 4) * 2 + n % 2) * GROUP
        return pl.ds(pl.multiple_of(first, 128), GROUP)

    local = []
    for index, (src, dst) in enumerate(
        (
            (q_hbm, q),
            (k_hbm, kw.at[1024:1536]),
            (v_hbm, vw.at[1024:1536]),
            (gy_hbm, cot.at[own_rows]),
            (w_hbm, w),
        )
    ):
        copy = pltpu.make_async_copy(src, dst, local_sem.at[index])
        copy.start()
        local.append(copy)

    barrier = pltpu.get_barrier_semaphore()
    peers = [core_dev, far_dev, lo_dev]
    peers += [x_dev(s) for s in (1, 2, 3)] + [z_dev(s) for s in (1, 2, 3)]
    peers += [c_dev(s) for s in (1, 2, -1, -2)]
    for peer in peers:
        pl.semaphore_signal(barrier, inc=1, device_id=peer, device_id_type=MESH)
    pl.semaphore_wait(barrier, len(peers))

    kv = []
    for src, dst, base in ((k_hbm, kw, 0), (v_hbm, vw, 2)):
        for step in (1, 2):
            slot = base + step - 1
            kv.append(
                send(
                    src,
                    dst.at[(2 - step) * 512 : (3 - step) * 512],
                    kv_ss.at[slot],
                    kv_rs.at[slot],
                    c_dev(step),
                )
            )
    gathers = []
    for n in range(8):
        cols = group_cols(n)
        gathers.append(
            send(gy_hbm.at[:, cols], cot.at[own_rows, cols], ag_ss.at[n], ag_rs.at[n], far_dev)
        )
    own_copy = send(gy_hbm, cot.at[own_rows], own_ss.at[0], own_rs.at[0], core_dev)

    scale = E ** (-0.5)
    log2e = scale * math.log2(math.e)

    def mask_bias(tile, chunk):
        t = c * ROWS + tile * E + lax.broadcasted_iota(jnp.int32, (1, E), 1)
        start = jnp.zeros((1, E), jnp.int32)
        run = jnp.int32(0)
        for d in range(32):
            run = run + lengths[d]
            start = jnp.where(t >= run, run, start)
        return t, start

    def visible(t, start, tile, chunk):
        j = (c - 2) * ROWS + tile * E + chunk * E + lax.broadcasted_iota(jnp.int32, (E, E), 0)
        bias = jnp.where((j >= start) & (j <= t), 0.0, MASKED)
        return jnp.concatenate([bias] * RATIO, axis=1)

    local[0].wait()
    local[1].wait()
    kv[0].wait_recv()
    kv[1].wait_recv()

    def weigh(tile, carry):
        first = pl.multiple_of(tile * E, E)
        t, start = mask_bias(tile, 0)
        qt = stack_heads(q, first)
        scores[...] = dot(kw[pl.ds(first, WIDTH), :], qt, NT)

        def largest(chunk, top):
            rows = pl.ds(pl.multiple_of(chunk * E, E), E)
            s = scores[rows, :] + visible(t, start, tile, chunk)
            scores[rows, :] = s
            return jnp.maximum(top, jnp.max(s.reshape(16, 8, COLS), axis=0))

        top = lax.fori_loop(0, 9, largest, jnp.full((8, COLS), MASKED, F32))
        top = jnp.max(top, axis=0, keepdims=True)

        def powers(chunk, total):
            rows = pl.ds(pl.multiple_of(chunk * E, E), E)
            p = jnp.exp2((scores[rows, :] - top) * log2e)
            scores[rows, :] = p
            return total + jnp.sum(p.reshape(16, 8, COLS), axis=0)

        total = lax.fori_loop(0, 9, powers, jnp.zeros((8, COLS), F32))
        inverse = 1.0 / jnp.sum(total, axis=0, keepdims=True)

        def normal(chunk, carry):
            rows = pl.ds(pl.multiple_of(chunk * E, E), E)
            probs[tile, rows, :] = (scores[rows, :] * inverse).astype(BF16)
            return carry

        lax.fori_loop(0, 9, normal, 0)
        return carry

    lax.fori_loop(0, 4, weigh, 0)
    local[2].wait()
    kv[2].wait_recv()
    kv[3].wait_recv()

    def attend(tile, carry):
        first = pl.multiple_of(tile * E, E)
        out = dot(vw[pl.ds(first, WIDTH), :], probs[tile], TN)
        for r in range(RATIO):
            att[pl.ds(first, E), r * E : (r + 1) * E] = out[:, r * E : (r + 1) * E].T.astype(BF16)
        return carry

    lax.fori_loop(0, 4, attend, 0)

    forwards = []

    def forward(n):
        gathers[n].wait_recv()
        cols = group_cols(n)
        ref = cot.at[far_rows, cols]
        forwards.append(send(ref, ref, fw_ss.at[n], fw_rs.at[n], core_dev))

    ax, bz = {}, {}

    def weight_group(n):
        forwards[n].wait_recv()
        step = Z_STEPS[n // 2]
        stage[n] = dot(cot[:, group_cols(n)], att[...], TN).astype(BF16)
        if n % 2 == 0:
            for dx in (2, 1, 3):
                first = pl.multiple_of(((x + dx) % 4) * PIECE, 32)
                slot = (n // 2) * 3 + dx - 1
                ax[n // 2, dx] = send(
                    stage.at[n, pl.ds(first, PIECE)],
                    ax_recv.at[slot],
                    ax_ss.at[slot],
                    ax_rs.at[slot],
                    x_dev(dx),
                )
        elif step:
            bz[step] = send(
                stage.at[n],
                bz_recv.at[step - 1],
                bz_ss.at[step - 1],
                bz_rs.at[step - 1],
                z_dev(step),
            )

    local[3].wait()
    own_copy.wait_recv()
    for n in range(4):
        forward(n)
    for n in range(4):
        weight_group(n)

    local[4].wait()

    def project(n, carry):
        first = pl.multiple_of(n * GROUP, 128)
        part[:, pl.ds(first, GROUP)] = dot(att[...], w[pl.ds(first, GROUP), :], NT).astype(BF16)
        return carry

    lax.fori_loop(0, 8, project, 0)
    to_core = {}
    for far in (1, 0):
        head = (h_core + 2 * far) % 4
        to_core[far] = send(
            part.at[rows_of(head)], core_recv.at[far], pc_ss.at[far], pc_rs.at[far], core_dev
        )
    for n in range(4, 6):
        forward(n)
    for n in range(4, 6):
        weight_group(n)
    to_core[1].wait_recv()
    to_far = []
    for n in range(4):
        cols = pl.ds(n * 1280, 1280)
        y_send[:, cols] = (part[far_rows, cols].astype(F32) + core_recv[1, :, cols].astype(F32)).astype(
            BF16
        )
        to_far.append(send(y_send.at[:, cols], y_recv.at[:, cols], py_ss.at[n], py_rs.at[n], far_dev))
    for n in range(6, 8):
        forward(n)
    for n in range(6, 8):
        weight_group(n)

    up_acc[...] = jnp.zeros_like(up_acc)

    def raise_up(n, carry):
        first = pl.multiple_of(n * GROUP, 128)
        up_acc[...] += dot(cot[:, pl.ds(first, GROUP)], w[pl.ds(first, GROUP), :], NN)
        return carry

    lax.fori_loop(0, 8, raise_up, 0)
    up[...] = up_acc[...].astype(BF16)

    az = {}

    def sum_x(index):
        step = Z_STEPS[index]
        first = pl.multiple_of(x * PIECE, 32)
        total = stage[2 * index, pl.ds(first, PIECE), :].astype(F32)
        for dx in (1, 2, 3):
            ax[index, dx].wait_recv()
            total = total + ax_recv[index * 3 + dx - 1].astype(F32)
        if step:
            az_send[step - 1] = total.astype(BF16)
            az[step] = send(
                az_send.at[step - 1],
                az_recv.at[step - 1],
                az_ss.at[step - 1],
                az_rs.at[step - 1],
                z_dev(step),
            )
        return total

    sum_x(0)
    sum_x(1)

    dk_acc[...] = jnp.zeros_like(dk_acc)
    dv_acc[...] = jnp.zeros_like(dv_acc)

    def backward(tile, carry):
        first = pl.multiple_of(tile * E, E)
        window = pl.ds(first, WIDTH)
        up_t = stack_heads(up, first)
        delta = []
        for r in range(RATIO):
            cols = slice(r * E, (r + 1) * E)
            prod = up[pl.ds(first, E), cols].astype(F32) * att[pl.ds(first, E), cols].astype(F32)
            delta.append(jnp.sum(prod.T, axis=0, keepdims=True))
        delta = jnp.concatenate(delta, axis=1)
        scores[...] = dot(vw[window, :], up_t, NT)
        dv_acc[window, :] += dot(probs[tile], up_t, NN)

        def grad(chunk, carry):
            rows = pl.ds(pl.multiple_of(chunk * E, E), E)
            weight = probs[tile, rows, :].astype(F32)
            probs[tile, rows, :] = (weight * (scores[rows, :] - delta)).astype(BF16)
            return carry

        lax.fori_loop(0, 9, grad, 0)
        dk_acc[window, :] += dot(probs[tile], stack_heads(q, first), NN)
        dq = dot(kw[window, :], probs[tile], TN) * scale
        for r in range(RATIO):
            dq_out[pl.ds(first, E), r * E : (r + 1) * E] = dq[:, r * E : (r + 1) * E].T.astype(BF16)
        return carry

    lax.fori_loop(0, 4, backward, 0)
    homes = []
    for index, acc in enumerate((dk_acc, dv_acc)):
        factor = scale if index == 0 else 1.0
        for step in (2, 1):
            slot = index * 2 + step - 1
            home_send[slot] = (acc[(2 - step) * 512 : (3 - step) * 512, :] * factor).astype(BF16)
            homes.append(
                send(
                    home_send.at[slot],
                    home_recv.at[slot],
                    home_ss.at[slot],
                    home_rs.at[slot],
                    c_dev(-step),
                )
            )

    sum_x(2)
    total_a = sum_x(3)
    for dz in (1, 2, 3):
        bz[dz].wait_recv()

    def sum_z(dx):
        rows = pl.ds(pl.multiple_of(((x + dx) % 4) * PIECE, 32), PIECE)
        total = stage[7, rows, :].astype(F32)
        for dz in (1, 2, 3):
            total = total + bz_recv[dz - 1, rows, :].astype(F32)
        return total

    bx = {}
    for dx in (2, 1, 3):
        bx_send[dx - 1] = sum_z(dx).astype(BF16)
        bx[dx] = send(
            bx_send.at[dx - 1], bx_recv.at[dx - 1], bx_ss.at[dx - 1], bx_rs.at[dx - 1], x_dev(dx)
        )
    total_b = sum_z(0)
    for dz in (1, 2, 3):
        az[dz].wait_recv()
        total_a = total_a + az_recv[dz - 1].astype(F32)
    for dx in (1, 2, 3):
        bx[dx].wait_recv()
        total_b = total_b + bx_recv[dx - 1].astype(F32)
    lower = yl == 0
    l_send[...] = jnp.where(lower, total_b, total_a).astype(BF16)
    last = send(l_send, l_recv, l_ss.at[0], l_rs.at[0], lo_dev)

    for copy in homes:
        copy.wait_recv()
    for index, (acc, out) in enumerate(((dk_acc, dk_out), (dv_acc, dv_out))):
        factor = scale if index == 0 else 1.0
        total = acc[1024:1536, :] * factor
        for step in (1, 2):
            total = total + home_recv[index * 2 + step - 1].astype(F32)
        out[...] = total.astype(BF16)

    to_core[0].wait_recv()
    for n in range(4):
        cols = pl.ds(n * 1280, 1280)
        to_far[n].wait_recv()
        proj_out[:, cols] = (
            part[own_rows, cols].astype(F32)
            + core_recv[0, :, cols].astype(F32)
            + y_recv[:, cols].astype(F32)
        ).astype(BF16)

    last.wait_recv()
    mine = jnp.where(lower, total_a, total_b)
    gw_out[...] = (mine + l_recv[...].astype(F32)) * (1.0 / 128.0)
    for copy in sends:
        copy.wait_send()


def on_device(queries, keys, values, lengths, w_out, grad_y):
    hbm = pl.BlockSpec(memory_space=pl.ANY)
    vmem = pl.BlockSpec(memory_space=pltpu.VMEM)
    dma = lambda n: pltpu.SemaphoreType.DMA((n,))
    return pl.pallas_call(
        kernel,
        out_shape=(
            jax.ShapeDtypeStruct((128, MODEL), BF16),
            jax.ShapeDtypeStruct((ROWS, COLS), BF16),
            jax.ShapeDtypeStruct((ROWS, E), BF16),
            jax.ShapeDtypeStruct((ROWS, E), BF16),
            jax.ShapeDtypeStruct((PIECE, COLS), F32),
        ),
        in_specs=[hbm, hbm, hbm, pl.BlockSpec(memory_space=pltpu.SMEM), hbm, hbm],
        out_specs=(vmem,) * 5,
        scratch_shapes=[
            pltpu.VMEM((ROWS, COLS), BF16),
            pltpu.VMEM((3 * ROWS, E), BF16),
            pltpu.VMEM((3 * ROWS, E), BF16),
            pltpu.VMEM((MODEL, COLS), BF16),
            pltpu.VMEM((ROWS, MODEL), BF16),
            pltpu.VMEM((ROWS, COLS), BF16),
            pltpu.VMEM((ROWS, COLS), BF16),
            pltpu.VMEM((ROWS, COLS), F32),
            pltpu.VMEM((4, WIDTH, COLS), BF16),
            pltpu.VMEM((WIDTH, COLS), F32),
            pltpu.VMEM((3 * ROWS, E), F32),
            pltpu.VMEM((3 * ROWS, E), F32),
            pltpu.VMEM((4, ROWS, E), BF16),
            pltpu.VMEM((4, ROWS, E), BF16),
            pltpu.VMEM((ROWS, MODEL), BF16),
            pltpu.VMEM((2, 128, MODEL), BF16),
            pltpu.VMEM((128, MODEL), BF16),
            pltpu.VMEM((128, MODEL), BF16),
            pltpu.VMEM((8, GROUP, COLS), BF16),
            pltpu.VMEM((12, PIECE, COLS), BF16),
            pltpu.VMEM((3, PIECE, COLS), BF16),
            pltpu.VMEM((3, PIECE, COLS), BF16),
            pltpu.VMEM((3, GROUP, COLS), BF16),
            pltpu.VMEM((3, PIECE, COLS), BF16),
            pltpu.VMEM((3, PIECE, COLS), BF16),
            pltpu.VMEM((PIECE, COLS), BF16),
            pltpu.VMEM((PIECE, COLS), BF16),
            dma(5),
            dma(4),
            dma(4),
            dma(1),
            dma(1),
            dma(8),
            dma(8),
            dma(8),
            dma(8),
            dma(4),
            dma(4),
            dma(2),
            dma(2),
            dma(4),
            dma(4),
            dma(12),
            dma(12),
            dma(3),
            dma(3),
            dma(3),
            dma(3),
            dma(3),
            dma(3),
            dma(1),
            dma(1),
        ],
        compiler_params=pltpu.CompilerParams(
            collective_id=0, has_side_effects=True, vmem_limit_bytes=63 << 20
        ),
    )(queries, keys, values, lengths, w_out, grad_y)


def solution(mesh):
    in_specs = (
        P("ctx", "head"),
        P("ctx", "head"),
        P("ctx", "head"),
        P(),
        P(None, "head"),
        P(("ctx", "head"), None),
    )
    out_specs = (
        P(("ctx", "head"), None),
        P("ctx", "head"),
        P("ctx", "head"),
        P("ctx", "head"),
        P("ctx", "head"),
    )
    return jax.shard_map(
        on_device, mesh=mesh, in_specs=in_specs, out_specs=out_specs, check_vma=False
    )
```

```python
import functools
import math

import jax
import jax.numpy as jnp
from jax import lax
from jax.experimental import pallas as pl
from jax.experimental.pallas import tpu as pltpu
from jax.sharding import PartitionSpec as P

E = 128
MESH = pl.DeviceIdType.MESH
F32 = jnp.float32
BF16 = jnp.bfloat16
NT = (((1,), (1,)), ((), ()))
TN = (((0,), (0,)), ((), ()))
NN = (((1,), (0,)), ((), ()))
RATIO = 5
ROWS = 512
COLS = RATIO * E
WIDTH = 9 * E
MODEL = 5120
GROUP = 640
PIECE = 160
MASKED = -1e30
Z_STEPS = (2, 1, 3, 0)


def dot(a, b, dims):
    return lax.dot_general(a, b, dims, preferred_element_type=F32)


def stack_heads(ref, first):
    return jnp.concatenate(
        [ref[pl.ds(first, E), r * E : (r + 1) * E] for r in range(RATIO)], axis=0
    )


def kernel(
    q_hbm,
    k_hbm,
    v_hbm,
    lengths,
    w_hbm,
    gy_hbm,
    proj_hbm,
    dq_hbm,
    dk_hbm,
    dv_hbm,
    gw_hbm,
    proj_out,
    dq_out,
    dk_out,
    dv_out,
    gw_out,
    q,
    kw,
    vw,
    kv_relay,
    w,
    cot,
    att,
    up,
    up_acc,
    probs,
    scores,
    dk_acc,
    dv_acc,
    home_send,
    home_recv,
    part,
    core_recv,
    y_send,
    y_recv,
    stage,
    ax_recv,
    az_send,
    az_recv,
    bz_recv,
    bx_send,
    bx_recv,
    l_send,
    l_recv,
    local_sem,
    out_sem,
    kv_ss,
    kv_rs,
    kr_ss,
    kr_rs,
    kf_ss,
    own_ss,
    own_rs,
    ag_ss,
    ag_rs,
    fw_ss,
    fw_rs,
    home_ss,
    home_rs,
    hp_ss,
    hp_rs,
    pc_ss,
    pc_rs,
    py_ss,
    py_rs,
    ax_ss,
    ax_rs,
    az_ss,
    az_rs,
    bz_ss,
    bz_rs,
    bx_ss,
    bx_rs,
    l_ss,
    l_rs,
):
    c = lax.axis_index("ctx")
    h = lax.axis_index("head")
    z, yl, x = c // 8, (c // 4) % 2, c % 4
    core, yh = h % 2, h // 2
    h_core = h + 1 - 2 * core
    h_far = (h + 2) % 4
    core_dev = (c, h_core)
    far_dev = (c, h_far)
    lo_dev = (c + 4 - 8 * yl, h)

    def x_dev(step):
        return (c - x + (x + step) % 4, h)

    def z_dev(step):
        return ((c + 8 * step) % 32, h)

    def c_dev(step):
        return ((c + step + 32) % 32, h)

    sends = []

    def remote(src, dst, ss, rs, device):
        return pltpu.make_async_remote_copy(
            src_ref=src, dst_ref=dst, send_sem=ss, recv_sem=rs, device_id=device, device_id_type=MESH
        )

    def send(src, dst, ss, rs, device):
        copy = remote(src, dst, ss, rs, device)
        copy.start()
        sends.append(copy)
        return copy

    def rows_of(head):
        return pl.ds(pl.multiple_of(head * 128, 128), 128)

    own_rows = rows_of(h)
    far_rows = rows_of(h_far)

    def group_cols(n):
        first = (((z + Z_STEPS[n // 2]) % 4) * 2 + n % 2) * GROUP
        return pl.ds(pl.multiple_of(first, 128), GROUP)

    local = []
    for index, (src, dst) in enumerate(
        (
            (q_hbm, q),
            (k_hbm, kw.at[1024:1536]),
            (v_hbm, vw.at[1024:1536]),
            (gy_hbm, cot.at[own_rows]),
            (w_hbm, w),
        )
    ):
        copy = pltpu.make_async_copy(src, dst, local_sem.at[index])
        copy.start()
        local.append(copy)

    barrier = pltpu.get_barrier_semaphore()
    peers = [core_dev, far_dev, lo_dev]
    peers += [x_dev(s) for s in (1, 2, 3)] + [z_dev(s) for s in (1, 2, 3)]
    peers += [c_dev(s) for s in (1, 2, 3, 4, -1, -2, -3, -4)]
    for peer in peers:
        pl.semaphore_signal(barrier, inc=1, device_id=peer, device_id_type=MESH)
    pl.semaphore_wait(barrier, len(peers))

    near, far, relays, hops = [], [], [], []
    for index, (src, dst) in enumerate(((k_hbm, kw), (v_hbm, vw))):
        near_dst, far_dst, relay = dst.at[512:1024], dst.at[0:512], kv_relay.at[index]
        near_sem, far_sem = kv_rs.at[2 * index], kv_rs.at[2 * index + 1]
        near.append(remote(src, near_dst, kv_ss.at[2 * index], near_sem, c_dev(1)))
        far.append(remote(src, far_dst, kv_ss.at[2 * index + 1], far_sem, c_dev(2)))
        relays.append(remote(src, relay, kr_ss.at[index], kr_rs.at[index], c_dev(4)))
        hops.append(
            (
                remote(relay, near_dst, kf_ss.at[2 * index], near_sem, c_dev(-3)),
                remote(relay, far_dst, kf_ss.at[2 * index + 1], far_sem, c_dev(-2)),
            )
        )

    @pl.when(x >= 2)
    def _():
        relays[0].start()
        relays[1].start()

    for index in (0, 1):

        @pl.when(x != 3)
        def _():
            near[index].start()

        @pl.when(x < 2)
        def _():
            far[index].start()

    def pass_block(index):
        @pl.when(x >= 2)
        def _():
            relays[index].wait_recv()
            hops[index][1].start()

        @pl.when(x == 3)
        def _():
            hops[index][0].start()

    def receive_block(index):
        near[index].wait_recv()
        far[index].wait_recv()

    gathers = []
    for n in range(8):
        cols = group_cols(n)
        gathers.append(
            send(gy_hbm.at[:, cols], cot.at[own_rows, cols], ag_ss.at[n], ag_rs.at[n], far_dev)
        )
    own_copy = send(gy_hbm, cot.at[own_rows], own_ss.at[0], own_rs.at[0], core_dev)

    scale = E ** (-0.5)
    log2e = scale * math.log2(math.e)

    def mask_bias(tile, chunk):
        t = c * ROWS + tile * E + lax.broadcasted_iota(jnp.int32, (1, E), 1)
        start = jnp.zeros((1, E), jnp.int32)
        run = jnp.int32(0)
        for d in range(32):
            run = run + lengths[d]
            start = jnp.where(t >= run, run, start)
        return t, start

    def visible(t, start, tile, chunk):
        j = (c - 2) * ROWS + tile * E + chunk * E + lax.broadcasted_iota(jnp.int32, (E, E), 0)
        bias = jnp.where((j >= start) & (j <= t), 0.0, MASKED)
        return jnp.concatenate([bias] * RATIO, axis=1)

    local[0].wait()
    local[1].wait()
    pass_block(0)
    pass_block(1)
    receive_block(0)

    def weigh(tile, carry):
        first = pl.multiple_of(tile * E, E)
        t, start = mask_bias(tile, 0)
        qt = stack_heads(q, first)
        scores[...] = dot(kw[pl.ds(first, WIDTH), :], qt, NT)

        def largest(chunk, top):
            rows = pl.ds(pl.multiple_of(chunk * E, E), E)
            s = scores[rows, :] + visible(t, start, tile, chunk)
            scores[rows, :] = s
            return jnp.maximum(top, jnp.max(s.reshape(16, 8, COLS), axis=0))

        top = lax.fori_loop(0, 9, largest, jnp.full((8, COLS), MASKED, F32))
        top = jnp.max(top, axis=0, keepdims=True)

        def powers(chunk, total):
            rows = pl.ds(pl.multiple_of(chunk * E, E), E)
            p = jnp.exp2((scores[rows, :] - top) * log2e)
            scores[rows, :] = p
            return total + jnp.sum(p.reshape(16, 8, COLS), axis=0)

        total = lax.fori_loop(0, 9, powers, jnp.zeros((8, COLS), F32))
        inverse = 1.0 / jnp.sum(total, axis=0, keepdims=True)

        def normal(chunk, carry):
            rows = pl.ds(pl.multiple_of(chunk * E, E), E)
            probs[tile, rows, :] = (scores[rows, :] * inverse).astype(BF16)
            return carry

        lax.fori_loop(0, 9, normal, 0)
        return carry

    lax.fori_loop(0, 4, weigh, 0)
    local[2].wait()
    receive_block(1)

    def attend(tile, carry):
        first = pl.multiple_of(tile * E, E)
        out = dot(vw[pl.ds(first, WIDTH), :], probs[tile], TN)
        for r in range(RATIO):
            att[pl.ds(first, E), r * E : (r + 1) * E] = out[:, r * E : (r + 1) * E].T.astype(BF16)
        return carry

    lax.fori_loop(0, 4, attend, 0)

    forwards = []

    def forward(n):
        gathers[n].wait_recv()
        cols = group_cols(n)
        ref = cot.at[far_rows, cols]
        forwards.append(send(ref, ref, fw_ss.at[n], fw_rs.at[n], core_dev))

    ax, bz = {}, {}

    def block_rows(step, first, count):
        return pl.ds(pl.multiple_of(((x + step) % 4) * PIECE + first, 16), count)

    def weight_group(n):
        forwards[n].wait_recv()
        step = Z_STEPS[n // 2]
        stage[n] = dot(cot[:, group_cols(n)], att[...], TN).astype(BF16)
        if n % 2 == 0:
            for dx in (2, 1, 3):
                slot = (n // 2) * 3 + dx - 1
                ax[n // 2, dx] = send(
                    stage.at[n, block_rows(dx, 0, PIECE)],
                    ax_recv.at[slot],
                    ax_ss.at[slot],
                    ax_rs.at[slot],
                    x_dev(dx),
                )
        elif step:
            bz[step] = send(
                stage.at[n],
                bz_recv.at[step - 1],
                bz_ss.at[step - 1],
                bz_rs.at[step - 1],
                z_dev(step),
            )

    def raise_up(pair):
        first = pl.multiple_of(((z + Z_STEPS[pair]) % 4) * 2 * GROUP, 128)
        columns = pl.ds(first, 2 * GROUP)
        more = dot(cot[:, columns], w[columns, :], NN)
        up_acc[...] = more if pair == 0 else up_acc[...] + more

    local[3].wait()
    own_copy.wait_recv()
    for n in range(4):
        forward(n)
    for n in range(4):
        weight_group(n)

    local[4].wait()

    def project(n, carry):
        first = pl.multiple_of(n * GROUP, 128)
        part[:, pl.ds(first, GROUP)] = dot(att[...], w[pl.ds(first, GROUP), :], NT).astype(BF16)
        return carry

    lax.fori_loop(0, 8, project, 0)
    to_core = {}
    for side in (1, 0):
        head = (h_core + 2 * side) % 4
        to_core[side] = send(
            part.at[rows_of(head)], core_recv.at[side], pc_ss.at[side], pc_rs.at[side], core_dev
        )
    raise_up(0)
    raise_up(1)
    for n in range(4, 6):
        forward(n)
    for n in range(4, 6):
        weight_group(n)
    to_core[1].wait_recv()
    to_far = []

    def sum_core(n):
        cols = pl.ds(n * 1280, 1280)
        y_send[:, cols] = (part[far_rows, cols].astype(F32) + core_recv[1, :, cols].astype(F32)).astype(
            BF16
        )
        to_far.append(send(y_send.at[:, cols], y_recv.at[:, cols], py_ss.at[n], py_rs.at[n], far_dev))

    sum_core(0)
    raise_up(2)
    for n in range(6, 8):
        forward(n)
    for n in range(1, 4):
        sum_core(n)
    for n in range(6, 8):
        weight_group(n)
    raise_up(3)
    up[...] = up_acc[...].astype(BF16)

    az = {}

    def sum_x(index):
        step = Z_STEPS[index]
        total = stage[2 * index, block_rows(0, 0, PIECE), :].astype(F32)
        for dx in (1, 2, 3):
            ax[index, dx].wait_recv()
            total = total + ax_recv[index * 3 + dx - 1].astype(F32)
        if step:
            az_send[step - 1] = total.astype(BF16)
            az[step] = send(
                az_send.at[step - 1],
                az_recv.at[step - 1],
                az_ss.at[step - 1],
                az_rs.at[step - 1],
                z_dev(step),
            )
        return total

    sum_x(0)

    dk_acc[...] = jnp.zeros_like(dk_acc)
    dv_acc[...] = jnp.zeros_like(dv_acc)

    def home_piece(index, tile):
        rows = pl.ds(pl.multiple_of(tile * E, E), E)
        slot = index * 2 + 1
        return remote(
            home_send.at[slot, rows],
            home_recv.at[slot, rows],
            hp_ss.at[index, tile],
            hp_rs.at[index, tile],
            c_dev(-2),
        )

    def backward(tile, carry):
        first = pl.multiple_of(tile * E, E)
        window = pl.ds(first, WIDTH)
        up_t = stack_heads(up, first)
        delta = []
        for r in range(RATIO):
            cols = slice(r * E, (r + 1) * E)
            prod = up[pl.ds(first, E), cols].astype(F32) * att[pl.ds(first, E), cols].astype(F32)
            delta.append(jnp.sum(prod.T, axis=0, keepdims=True))
        delta = jnp.concatenate(delta, axis=1)
        scores[...] = dot(vw[window, :], up_t, NT)
        dv_acc[window, :] += dot(probs[tile], up_t, NN)

        def grad(chunk, carry):
            rows = pl.ds(pl.multiple_of(chunk * E, E), E)
            weight = probs[tile, rows, :].astype(F32)
            probs[tile, rows, :] = (weight * (scores[rows, :] - delta)).astype(BF16)
            return carry

        lax.fori_loop(0, 9, grad, 0)
        dk_acc[window, :] += dot(probs[tile], stack_heads(q, first), NN)
        rows = pl.ds(first, E)
        home_send[1, rows] = (dk_acc[rows, :] * scale).astype(BF16)
        home_send[3, rows] = dv_acc[rows, :].astype(BF16)
        for index in (0, 1):
            home_piece(index, tile).start()
        dq = dot(kw[window, :], probs[tile], TN) * scale
        for r in range(RATIO):
            dq_out[pl.ds(first, E), r * E : (r + 1) * E] = dq[:, r * E : (r + 1) * E].T.astype(BF16)
        return carry

    lax.fori_loop(0, 2, backward, 0)
    sum_x(1)
    lax.fori_loop(2, 4, backward, 0)
    homes = [home_piece(index, tile) for index in (0, 1) for tile in range(4)]
    sends.extend(homes)
    for index, acc in enumerate((dk_acc, dv_acc)):
        factor = scale if index == 0 else 1.0
        slot = index * 2
        home_send[slot] = (acc[512:1024, :] * factor).astype(BF16)
        homes.append(
            send(
                home_send.at[slot],
                home_recv.at[slot],
                home_ss.at[index],
                home_rs.at[index],
                c_dev(-1),
            )
        )

    outs = []

    def write(index, src, dst):
        copy = pltpu.make_async_copy(src, dst, out_sem.at[index])
        copy.start()
        outs.append(copy)

    write(0, dq_out, dq_hbm)
    sum_x(2)
    total_a = sum_x(3)
    for dz in (1, 2, 3):
        bz[dz].wait_recv()

    def sum_z(step):
        rows = block_rows(step, 0, PIECE)
        total = stage[7, rows, :].astype(F32)
        for dz in (1, 2, 3):
            total = total + bz_recv[dz - 1, rows, :].astype(F32)
        return total

    bx = {}
    for dx in (2, 1, 3):
        bx_send[dx - 1] = sum_z(dx).astype(BF16)
        bx[dx] = send(
            bx_send.at[dx - 1], bx_recv.at[dx - 1], bx_ss.at[dx - 1], bx_rs.at[dx - 1], x_dev(dx)
        )
    total_b = sum_z(0)
    for dz in (1, 2, 3):
        az[dz].wait_recv()
        total_a = total_a + az_recv[dz - 1].astype(F32)
    for dx in (1, 2, 3):
        bx[dx].wait_recv()
        total_b = total_b + bx_recv[dx - 1].astype(F32)
    lower = yl == 0
    l_send[...] = jnp.where(lower, total_b, total_a).astype(BF16)
    last = send(l_send, l_recv, l_ss.at[0], l_rs.at[0], lo_dev)

    for copy in homes:
        copy.wait_recv()
    for index, (acc, out) in enumerate(((dk_acc, dk_out), (dv_acc, dv_out))):
        factor = scale if index == 0 else 1.0
        total = acc[1024:1536, :] * factor
        for step in (1, 2):
            total = total + home_recv[index * 2 + step - 1].astype(F32)
        out[...] = total.astype(BF16)
        write(1 + index, out, (dk_hbm, dv_hbm)[index])

    to_core[0].wait_recv()
    for n in range(4):
        cols = pl.ds(n * 1280, 1280)
        to_far[n].wait_recv()
        proj_out[:, cols] = (
            part[own_rows, cols].astype(F32)
            + core_recv[0, :, cols].astype(F32)
            + y_recv[:, cols].astype(F32)
        ).astype(BF16)
        write(3 + n, proj_out.at[:, cols], proj_hbm.at[:, cols])

    last.wait_recv()
    mine = jnp.where(lower, total_a, total_b)
    gw_out[...] = (mine + l_recv[...].astype(F32)) * (1.0 / 128.0)
    write(7, gw_out, gw_hbm)
    for copy in sends:
        copy.wait_send()
    for index in (0, 1):

        @pl.when(x != 3)
        def _():
            near[index].wait_send()

        @pl.when(x < 2)
        def _():
            far[index].wait_send()

        @pl.when(x >= 2)
        def _():
            relays[index].wait_send()
            hops[index][1].wait_send()

        @pl.when(x == 3)
        def _():
            hops[index][0].wait_send()

    for copy in outs:
        copy.wait()


def keep(*refs):
    for src, dst in zip(refs[:5], refs[5:]):
        dst[...] = src[...]


def on_device(queries, keys, values, lengths, w_out, grad_y):
    hbm = pl.BlockSpec(memory_space=pl.ANY)
    vmem = pl.BlockSpec(memory_space=pltpu.VMEM)
    dma = lambda *n: pltpu.SemaphoreType.DMA(n)
    shapes = (
            jax.ShapeDtypeStruct((128, MODEL), BF16),
            jax.ShapeDtypeStruct((ROWS, COLS), BF16),
            jax.ShapeDtypeStruct((ROWS, E), BF16),
            jax.ShapeDtypeStruct((ROWS, E), BF16),
            jax.ShapeDtypeStruct((PIECE, COLS), F32),
    )
    results = pl.pallas_call(
        kernel,
        out_shape=shapes,
        in_specs=[hbm, hbm, hbm, pl.BlockSpec(memory_space=pltpu.SMEM), hbm, hbm],
        out_specs=(hbm,) * 5,
        scratch_shapes=[
            *[pltpu.VMEM(s.shape, s.dtype) for s in shapes],
            pltpu.VMEM((ROWS, COLS), BF16),
            pltpu.VMEM((3 * ROWS, E), BF16),
            pltpu.VMEM((3 * ROWS, E), BF16),
            pltpu.VMEM((2, ROWS, E), BF16),
            pltpu.VMEM((MODEL, COLS), BF16),
            pltpu.VMEM((ROWS, MODEL), BF16),
            pltpu.VMEM((ROWS, COLS), BF16),
            pltpu.VMEM((ROWS, COLS), BF16),
            pltpu.VMEM((ROWS, COLS), F32),
            pltpu.VMEM((4, WIDTH, COLS), BF16),
            pltpu.VMEM((WIDTH, COLS), F32),
            pltpu.VMEM((3 * ROWS, E), F32),
            pltpu.VMEM((3 * ROWS, E), F32),
            pltpu.VMEM((4, ROWS, E), BF16),
            pltpu.VMEM((4, ROWS, E), BF16),
            pltpu.VMEM((ROWS, MODEL), BF16),
            pltpu.VMEM((2, 128, MODEL), BF16),
            pltpu.VMEM((128, MODEL), BF16),
            pltpu.VMEM((128, MODEL), BF16),
            pltpu.VMEM((8, GROUP, COLS), BF16),
            pltpu.VMEM((12, PIECE, COLS), BF16),
            pltpu.VMEM((3, PIECE, COLS), BF16),
            pltpu.VMEM((3, PIECE, COLS), BF16),
            pltpu.VMEM((3, GROUP, COLS), BF16),
            pltpu.VMEM((3, PIECE, COLS), BF16),
            pltpu.VMEM((3, PIECE, COLS), BF16),
            pltpu.VMEM((PIECE, COLS), BF16),
            pltpu.VMEM((PIECE, COLS), BF16),
            dma(5),
            dma(8),
            dma(4),
            dma(4),
            dma(2),
            dma(2),
            dma(4),
            dma(1),
            dma(1),
            dma(8),
            dma(8),
            dma(8),
            dma(8),
            dma(2),
            dma(2),
            dma(2, 4),
            dma(2, 4),
            dma(2),
            dma(2),
            dma(4),
            dma(4),
            dma(12),
            dma(12),
            dma(3),
            dma(3),
            dma(3),
            dma(3),
            dma(3),
            dma(3),
            dma(1),
            dma(1),
        ],
        compiler_params=pltpu.CompilerParams(
            collective_id=0, has_side_effects=True, vmem_limit_bytes=63 << 20
        ),
    )(queries, keys, values, lengths, w_out, grad_y)
    return pl.pallas_call(
        keep, out_shape=shapes, in_specs=[vmem] * 5, out_specs=(vmem,) * 5
    )(*results)


def solution(mesh):
    in_specs = (
        P("ctx", "head"),
        P("ctx", "head"),
        P("ctx", "head"),
        P(),
        P(None, "head"),
        P(("ctx", "head"), None),
    )
    out_specs = (
        P(("ctx", "head"), None),
        P("ctx", "head"),
        P("ctx", "head"),
        P("ctx", "head"),
        P("ctx", "head"),
    )
    return jax.shard_map(
        on_device, mesh=mesh, in_specs=in_specs, out_specs=out_specs, check_vma=False
    )
```

```python
import functools
import math

import jax
import jax.numpy as jnp
from jax import lax
from jax.experimental import pallas as pl
from jax.experimental.pallas import tpu as pltpu
from jax.sharding import PartitionSpec as P

E = 128
MESH = pl.DeviceIdType.MESH
F32 = jnp.float32
BF16 = jnp.bfloat16
NT = (((1,), (1,)), ((), ()))
TN = (((0,), (0,)), ((), ()))
NN = (((1,), (0,)), ((), ()))
RATIO = 5
ROWS = 512
COLS = RATIO * E
WIDTH = 9 * E
MODEL = 5120
GROUP = 640
PIECE = 160
MASKED = -1e30
Z_STEPS = (2, 1, 3, 0)


def dot(a, b, dims):
    return lax.dot_general(a, b, dims, preferred_element_type=F32)


def stack_heads(ref, first):
    return jnp.concatenate(
        [ref[pl.ds(first, E), r * E : (r + 1) * E] for r in range(RATIO)], axis=0
    )


def kernel(
    q_hbm,
    k_hbm,
    v_hbm,
    lengths,
    w_hbm,
    gy_hbm,
    proj_hbm,
    dq_hbm,
    dk_hbm,
    dv_hbm,
    gw_hbm,
    proj_out,
    dq_out,
    dk_out,
    dv_out,
    gw_out,
    q,
    kw,
    vw,
    kv_relay,
    w,
    cot,
    att,
    up,
    up_acc,
    probs,
    scores,
    dk_acc,
    dv_acc,
    home_send,
    home_recv,
    part,
    core_recv,
    y_send,
    y_recv,
    stage,
    ax_recv,
    az_send,
    az_recv,
    bz_relay,
    bz_recv,
    bx_send,
    bx_recv,
    l_send,
    l_recv,
    local_sem,
    out_sem,
    kv_ss,
    kv_rs,
    kr_ss,
    kr_rs,
    kf_ss,
    own_ss,
    own_rs,
    ag_ss,
    ag_rs,
    fw_ss,
    fw_rs,
    home_ss,
    home_rs,
    hp_ss,
    hp_rs,
    pc_ss,
    pc_rs,
    py_ss,
    py_rs,
    ax_ss,
    ax_rs,
    az_ss,
    az_rs,
    br_ss,
    br_rs,
    bz_ss,
    bz_rs,
    bx_ss,
    bx_rs,
    l_ss,
    l_rs,
):
    c = lax.axis_index("ctx")
    h = lax.axis_index("head")
    z, yl, x = c // 8, (c // 4) % 2, c % 4
    core, yh = h % 2, h // 2
    h_core = h + 1 - 2 * core
    h_far = (h + 2) % 4
    core_dev = (c, h_core)
    far_dev = (c, h_far)
    lo_dev = (c + 4 - 8 * yl, h)

    def x_dev(step):
        return (c - x + (x + step) % 4, h)

    def z_dev(step):
        return ((c + 8 * step) % 32, h)

    def c_dev(step):
        return ((c + step + 32) % 32, h)

    sends = []

    def remote(src, dst, ss, rs, device):
        return pltpu.make_async_remote_copy(
            src_ref=src, dst_ref=dst, send_sem=ss, recv_sem=rs, device_id=device, device_id_type=MESH
        )

    def send(src, dst, ss, rs, device):
        copy = remote(src, dst, ss, rs, device)
        copy.start()
        sends.append(copy)
        return copy

    def rows_of(head):
        return pl.ds(pl.multiple_of(head * 128, 128), 128)

    own_rows = rows_of(h)
    far_rows = rows_of(h_far)

    def group_cols(n):
        first = (((z + Z_STEPS[n // 2]) % 4) * 2 + n % 2) * GROUP
        return pl.ds(pl.multiple_of(first, 128), GROUP)

    local = []
    for index, (src, dst) in enumerate(
        (
            (q_hbm, q),
            (k_hbm, kw.at[1024:1536]),
            (v_hbm, vw.at[1024:1536]),
            (gy_hbm, cot.at[own_rows]),
            (w_hbm, w),
        )
    ):
        copy = pltpu.make_async_copy(src, dst, local_sem.at[index])
        copy.start()
        local.append(copy)

    barrier = pltpu.get_barrier_semaphore()
    peers = [core_dev, far_dev, lo_dev]
    peers += [x_dev(s) for s in (1, 2, 3)] + [z_dev(s) for s in (1, 2, 3)]
    peers += [c_dev(s) for s in (1, 2, 3, 4, -1, -2, -3, -4)]
    for peer in peers:
        pl.semaphore_signal(barrier, inc=1, device_id=peer, device_id_type=MESH)
    pl.semaphore_wait(barrier, len(peers))

    near, far, relays, hops = [], [], [], []
    for index, (src, dst) in enumerate(((k_hbm, kw), (v_hbm, vw))):
        near_dst, far_dst, relay = dst.at[512:1024], dst.at[0:512], kv_relay.at[index]
        near_sem, far_sem = kv_rs.at[2 * index], kv_rs.at[2 * index + 1]
        near.append(remote(src, near_dst, kv_ss.at[2 * index], near_sem, c_dev(1)))
        far.append(remote(src, far_dst, kv_ss.at[2 * index + 1], far_sem, c_dev(2)))
        relays.append(remote(src, relay, kr_ss.at[index], kr_rs.at[index], c_dev(4)))
        hops.append(
            (
                remote(relay, near_dst, kf_ss.at[2 * index], near_sem, c_dev(-3)),
                remote(relay, far_dst, kf_ss.at[2 * index + 1], far_sem, c_dev(-2)),
            )
        )

    @pl.when(x >= 2)
    def _():
        relays[0].start()
        relays[1].start()

    for index in (0, 1):

        @pl.when(x != 3)
        def _():
            near[index].start()

        @pl.when(x < 2)
        def _():
            far[index].start()

    def pass_block(index):
        @pl.when(x >= 2)
        def _():
            relays[index].wait_recv()
            hops[index][1].start()

        @pl.when(x == 3)
        def _():
            hops[index][0].start()

    def receive_block(index):
        near[index].wait_recv()
        far[index].wait_recv()

    gathers = []
    for n in range(8):
        cols = group_cols(n)
        gathers.append(
            send(gy_hbm.at[:, cols], cot.at[own_rows, cols], ag_ss.at[n], ag_rs.at[n], far_dev)
        )
    own_copy = send(gy_hbm, cot.at[own_rows], own_ss.at[0], own_rs.at[0], core_dev)

    scale = E ** (-0.5)
    log2e = scale * math.log2(math.e)

    def mask_bias(tile, chunk):
        t = c * ROWS + tile * E + lax.broadcasted_iota(jnp.int32, (1, E), 1)
        start = jnp.zeros((1, E), jnp.int32)
        run = jnp.int32(0)
        for d in range(32):
            run = run + lengths[d]
            start = jnp.where(t >= run, run, start)
        return t, start

    def visible(t, start, tile, chunk):
        j = (c - 2) * ROWS + tile * E + chunk * E + lax.broadcasted_iota(jnp.int32, (E, E), 0)
        bias = jnp.where((j >= start) & (j <= t), 0.0, MASKED)
        return jnp.concatenate([bias] * RATIO, axis=1)

    local[0].wait()
    local[1].wait()
    pass_block(0)
    pass_block(1)
    receive_block(0)

    def weigh(tile, carry):
        first = pl.multiple_of(tile * E, E)
        t, start = mask_bias(tile, 0)
        qt = stack_heads(q, first)
        scores[...] = dot(kw[pl.ds(first, WIDTH), :], qt, NT)

        def largest(chunk, top):
            rows = pl.ds(pl.multiple_of(chunk * E, E), E)
            s = scores[rows, :] + visible(t, start, tile, chunk)
            scores[rows, :] = s
            return jnp.maximum(top, jnp.max(s.reshape(16, 8, COLS), axis=0))

        top = lax.fori_loop(0, 9, largest, jnp.full((8, COLS), MASKED, F32))
        top = jnp.max(top, axis=0, keepdims=True)

        def powers(chunk, total):
            rows = pl.ds(pl.multiple_of(chunk * E, E), E)
            p = jnp.exp2((scores[rows, :] - top) * log2e)
            scores[rows, :] = p
            return total + jnp.sum(p.reshape(16, 8, COLS), axis=0)

        total = lax.fori_loop(0, 9, powers, jnp.zeros((8, COLS), F32))
        inverse = 1.0 / jnp.sum(total, axis=0, keepdims=True)

        def normal(chunk, carry):
            rows = pl.ds(pl.multiple_of(chunk * E, E), E)
            probs[tile, rows, :] = (scores[rows, :] * inverse).astype(BF16)
            return carry

        lax.fori_loop(0, 9, normal, 0)
        return carry

    lax.fori_loop(0, 4, weigh, 0)
    local[2].wait()
    receive_block(1)

    def attend(tile, carry):
        first = pl.multiple_of(tile * E, E)
        out = dot(vw[pl.ds(first, WIDTH), :], probs[tile], TN)
        for r in range(RATIO):
            att[pl.ds(first, E), r * E : (r + 1) * E] = out[:, r * E : (r + 1) * E].T.astype(BF16)
        return carry

    lax.fori_loop(0, 4, attend, 0)

    forwards = []

    def forward(n):
        gathers[n].wait_recv()
        cols = group_cols(n)
        ref = cot.at[far_rows, cols]
        forwards.append(send(ref, ref, fw_ss.at[n], fw_rs.at[n], core_dev))

    ax, br, bz = {}, {}, {}

    def block_rows(step, first, count):
        return pl.ds(pl.multiple_of(((x + step) % 4) * PIECE + first, 16), count)

    def weight_group(n):
        forwards[n].wait_recv()
        step = Z_STEPS[n // 2]
        stage[n] = dot(cot[:, group_cols(n)], att[...], TN).astype(BF16)
        if n % 2 == 0:
            for dx in (2, 1, 3):
                slot = (n // 2) * 3 + dx - 1
                ax[n // 2, dx] = send(
                    stage.at[n, block_rows(dx, 0, PIECE)],
                    ax_recv.at[slot],
                    ax_ss.at[slot],
                    ax_rs.at[slot],
                    x_dev(dx),
                )
        elif step == 2:
            for dx in Z_STEPS:
                for way in (0, 1):
                    slot = 2 * dx + way
                    br[way, dx] = send(
                        stage.at[n, block_rows(dx, 80 * way, 80)],
                        bz_relay.at[slot],
                        br_ss.at[slot],
                        br_rs.at[slot],
                        z_dev((1, 3)[way]),
                    )

    def relay_z(way, dx):
        br[way, dx].wait_recv()
        rows = block_rows(dx, 80 * way, 80)
        slot = 2 * dx + way
        stage[2 * way + 3, rows, :] = (
            stage[2 * way + 3, rows, :].astype(F32) + bz_relay[slot].astype(F32)
        ).astype(BF16)
        whole = block_rows(dx, 0, PIECE)
        bz[way, dx] = send(
            stage.at[2 * way + 3, whole],
            bz_recv.at[way, whole],
            bz_ss.at[slot],
            bz_rs.at[slot],
            z_dev((1, 3)[way]),
        )

    def raise_up(pair):
        first = pl.multiple_of(((z + Z_STEPS[pair]) % 4) * 2 * GROUP, 128)
        columns = pl.ds(first, 2 * GROUP)
        more = dot(cot[:, columns], w[columns, :], NN)
        up_acc[...] = more if pair == 0 else up_acc[...] + more

    local[3].wait()
    own_copy.wait_recv()
    for n in range(4):
        forward(n)
    for n in range(4):
        weight_group(n)

    local[4].wait()

    def project(n, carry):
        first = pl.multiple_of(n * GROUP, 128)
        part[:, pl.ds(first, GROUP)] = dot(att[...], w[pl.ds(first, GROUP), :], NT).astype(BF16)
        return carry

    lax.fori_loop(0, 8, project, 0)
    to_core = {}
    for side in (1, 0):
        head = (h_core + 2 * side) % 4
        to_core[side] = send(
            part.at[rows_of(head)], core_recv.at[side], pc_ss.at[side], pc_rs.at[side], core_dev
        )
    for n in range(4, 6):
        forward(n)
    raise_up(0)
    raise_up(1)
    for dx in Z_STEPS:
        relay_z(0, dx)
    for n in (5, 4):
        weight_group(n)
    for dx in Z_STEPS:
        relay_z(1, dx)
    to_core[1].wait_recv()
    to_far = []

    def sum_core(n):
        cols = pl.ds(n * 1280, 1280)
        y_send[:, cols] = (part[far_rows, cols].astype(F32) + core_recv[1, :, cols].astype(F32)).astype(
            BF16
        )
        to_far.append(send(y_send.at[:, cols], y_recv.at[:, cols], py_ss.at[n], py_rs.at[n], far_dev))

    sum_core(0)
    raise_up(2)
    for n in range(6, 8):
        forward(n)
    for n in range(1, 4):
        sum_core(n)
    for n in range(6, 8):
        weight_group(n)
    raise_up(3)
    up[...] = up_acc[...].astype(BF16)

    az = {}

    def sum_x(index):
        step = Z_STEPS[index]
        total = stage[2 * index, block_rows(0, 0, PIECE), :].astype(F32)
        for dx in (1, 2, 3):
            ax[index, dx].wait_recv()
            total = total + ax_recv[index * 3 + dx - 1].astype(F32)
        if step:
            az_send[step - 1] = total.astype(BF16)
            az[step] = send(
                az_send.at[step - 1],
                az_recv.at[step - 1],
                az_ss.at[step - 1],
                az_rs.at[step - 1],
                z_dev(step),
            )
        return total

    bx = {}

    def sum_z(dx):
        rows = block_rows(dx, 0, PIECE)
        total = stage[7, rows, :].astype(F32)
        for way in (0, 1):
            bz[way, dx].wait_recv()
            total = total + bz_recv[way, rows, :].astype(F32)
        if dx:
            bx_send[dx - 1] = total.astype(BF16)
            bx[dx] = send(
                bx_send.at[dx - 1], bx_recv.at[dx - 1], bx_ss.at[dx - 1], bx_rs.at[dx - 1], x_dev(dx)
            )
        return total

    sum_x(0)

    dk_acc[...] = jnp.zeros_like(dk_acc)
    dv_acc[...] = jnp.zeros_like(dv_acc)

    def home_piece(index, tile):
        rows = pl.ds(pl.multiple_of(tile * E, E), E)
        slot = index * 2 + 1
        return remote(
            home_send.at[slot, rows],
            home_recv.at[slot, rows],
            hp_ss.at[index, tile],
            hp_rs.at[index, tile],
            c_dev(-2),
        )

    def backward(tile, carry):
        first = pl.multiple_of(tile * E, E)
        window = pl.ds(first, WIDTH)
        up_t = stack_heads(up, first)
        delta = []
        for r in range(RATIO):
            cols = slice(r * E, (r + 1) * E)
            prod = up[pl.ds(first, E), cols].astype(F32) * att[pl.ds(first, E), cols].astype(F32)
            delta.append(jnp.sum(prod.T, axis=0, keepdims=True))
        delta = jnp.concatenate(delta, axis=1)
        scores[...] = dot(vw[window, :], up_t, NT)
        dv_acc[window, :] += dot(probs[tile], up_t, NN)

        def grad(chunk, carry):
            rows = pl.ds(pl.multiple_of(chunk * E, E), E)
            weight = probs[tile, rows, :].astype(F32)
            probs[tile, rows, :] = (weight * (scores[rows, :] - delta)).astype(BF16)
            return carry

        lax.fori_loop(0, 9, grad, 0)
        dk_acc[window, :] += dot(probs[tile], stack_heads(q, first), NN)
        rows = pl.ds(first, E)
        home_send[1, rows] = (dk_acc[rows, :] * scale).astype(BF16)
        home_send[3, rows] = dv_acc[rows, :].astype(BF16)
        for index in (0, 1):
            home_piece(index, tile).start()
        dq = dot(kw[window, :], probs[tile], TN) * scale
        for r in range(RATIO):
            dq_out[pl.ds(first, E), r * E : (r + 1) * E] = dq[:, r * E : (r + 1) * E].T.astype(BF16)
        return carry

    lax.fori_loop(0, 1, backward, 0)
    sum_x(1)
    lax.fori_loop(1, 2, backward, 0)
    sum_z(2)
    lax.fori_loop(2, 3, backward, 0)
    sum_z(1)
    sum_x(2)
    lax.fori_loop(3, 4, backward, 0)
    sum_z(3)
    total_a = sum_x(3)
    total_b = sum_z(0)
    homes = [home_piece(index, tile) for index in (0, 1) for tile in range(4)]
    sends.extend(homes)
    for index, acc in enumerate((dk_acc, dv_acc)):
        factor = scale if index == 0 else 1.0
        slot = index * 2
        home_send[slot] = (acc[512:1024, :] * factor).astype(BF16)
        homes.append(
            send(
                home_send.at[slot],
                home_recv.at[slot],
                home_ss.at[index],
                home_rs.at[index],
                c_dev(-1),
            )
        )

    outs = []

    def write(index, src, dst):
        copy = pltpu.make_async_copy(src, dst, out_sem.at[index])
        copy.start()
        outs.append(copy)

    write(0, dq_out, dq_hbm)
    for dz in (1, 2, 3):
        az[dz].wait_recv()
        total_a = total_a + az_recv[dz - 1].astype(F32)
    for dx in (1, 2, 3):
        bx[dx].wait_recv()
        total_b = total_b + bx_recv[dx - 1].astype(F32)
    lower = yl == 0
    l_send[...] = jnp.where(lower, total_b, total_a).astype(BF16)
    last = send(l_send, l_recv, l_ss.at[0], l_rs.at[0], lo_dev)

    for copy in homes:
        copy.wait_recv()
    for index, (acc, out) in enumerate(((dk_acc, dk_out), (dv_acc, dv_out))):
        factor = scale if index == 0 else 1.0
        total = acc[1024:1536, :] * factor
        for step in (1, 2):
            total = total + home_recv[index * 2 + step - 1].astype(F32)
        out[...] = total.astype(BF16)
        write(1 + index, out, (dk_hbm, dv_hbm)[index])

    to_core[0].wait_recv()
    for n in range(4):
        cols = pl.ds(n * 1280, 1280)
        to_far[n].wait_recv()
        proj_out[:, cols] = (
            part[own_rows, cols].astype(F32)
            + core_recv[0, :, cols].astype(F32)
            + y_recv[:, cols].astype(F32)
        ).astype(BF16)
        write(3 + n, proj_out.at[:, cols], proj_hbm.at[:, cols])

    last.wait_recv()
    mine = jnp.where(lower, total_a, total_b)
    gw_out[...] = (mine + l_recv[...].astype(F32)) * (1.0 / 128.0)
    write(7, gw_out, gw_hbm)
    for copy in sends:
        copy.wait_send()
    for index in (0, 1):

        @pl.when(x != 3)
        def _():
            near[index].wait_send()

        @pl.when(x < 2)
        def _():
            far[index].wait_send()

        @pl.when(x >= 2)
        def _():
            relays[index].wait_send()
            hops[index][1].wait_send()

        @pl.when(x == 3)
        def _():
            hops[index][0].wait_send()

    for copy in outs:
        copy.wait()


def keep(*refs):
    for src, dst in zip(refs[:5], refs[5:]):
        dst[...] = src[...]


def on_device(queries, keys, values, lengths, w_out, grad_y):
    hbm = pl.BlockSpec(memory_space=pl.ANY)
    vmem = pl.BlockSpec(memory_space=pltpu.VMEM)
    dma = lambda *n: pltpu.SemaphoreType.DMA(n)
    shapes = (
            jax.ShapeDtypeStruct((128, MODEL), BF16),
            jax.ShapeDtypeStruct((ROWS, COLS), BF16),
            jax.ShapeDtypeStruct((ROWS, E), BF16),
            jax.ShapeDtypeStruct((ROWS, E), BF16),
            jax.ShapeDtypeStruct((PIECE, COLS), F32),
    )
    results = pl.pallas_call(
        kernel,
        out_shape=shapes,
        in_specs=[hbm, hbm, hbm, pl.BlockSpec(memory_space=pltpu.SMEM), hbm, hbm],
        out_specs=(hbm,) * 5,
        scratch_shapes=[
            *[pltpu.VMEM(s.shape, s.dtype) for s in shapes],
            pltpu.VMEM((ROWS, COLS), BF16),
            pltpu.VMEM((3 * ROWS, E), BF16),
            pltpu.VMEM((3 * ROWS, E), BF16),
            pltpu.VMEM((2, ROWS, E), BF16),
            pltpu.VMEM((MODEL, COLS), BF16),
            pltpu.VMEM((ROWS, MODEL), BF16),
            pltpu.VMEM((ROWS, COLS), BF16),
            pltpu.VMEM((ROWS, COLS), BF16),
            pltpu.VMEM((ROWS, COLS), F32),
            pltpu.VMEM((4, WIDTH, COLS), BF16),
            pltpu.VMEM((WIDTH, COLS), F32),
            pltpu.VMEM((3 * ROWS, E), F32),
            pltpu.VMEM((3 * ROWS, E), F32),
            pltpu.VMEM((4, ROWS, E), BF16),
            pltpu.VMEM((4, ROWS, E), BF16),
            pltpu.VMEM((ROWS, MODEL), BF16),
            pltpu.VMEM((2, 128, MODEL), BF16),
            pltpu.VMEM((128, MODEL), BF16),
            pltpu.VMEM((128, MODEL), BF16),
            pltpu.VMEM((8, GROUP, COLS), BF16),
            pltpu.VMEM((12, PIECE, COLS), BF16),
            pltpu.VMEM((3, PIECE, COLS), BF16),
            pltpu.VMEM((3, PIECE, COLS), BF16),
            pltpu.VMEM((8, 80, COLS), BF16),
            pltpu.VMEM((2, GROUP, COLS), BF16),
            pltpu.VMEM((3, PIECE, COLS), BF16),
            pltpu.VMEM((3, PIECE, COLS), BF16),
            pltpu.VMEM((PIECE, COLS), BF16),
            pltpu.VMEM((PIECE, COLS), BF16),
            dma(5),
            dma(8),
            dma(4),
            dma(4),
            dma(2),
            dma(2),
            dma(4),
            dma(1),
            dma(1),
            dma(8),
            dma(8),
            dma(8),
            dma(8),
            dma(2),
            dma(2),
            dma(2, 4),
            dma(2, 4),
            dma(2),
            dma(2),
            dma(4),
            dma(4),
            dma(12),
            dma(12),
            dma(3),
            dma(3),
            dma(8),
            dma(8),
            dma(8),
            dma(8),
            dma(3),
            dma(3),
            dma(1),
            dma(1),
        ],
        compiler_params=pltpu.CompilerParams(
            collective_id=0, has_side_effects=True, vmem_limit_bytes=63 << 20
        ),
    )(queries, keys, values, lengths, w_out, grad_y)
    return pl.pallas_call(
        keep, out_shape=shapes, in_specs=[vmem] * 5, out_specs=(vmem,) * 5
    )(*results)


def solution(mesh):
    in_specs = (
        P("ctx", "head"),
        P("ctx", "head"),
        P("ctx", "head"),
        P(),
        P(None, "head"),
        P(("ctx", "head"), None),
    )
    out_specs = (
        P(("ctx", "head"), None),
        P("ctx", "head"),
        P("ctx", "head"),
        P("ctx", "head"),
        P("ctx", "head"),
    )
    return jax.shard_map(
        on_device, mesh=mesh, in_specs=in_specs, out_specs=out_specs, check_vma=False
    )
```

```python
import functools
import math

import jax
import jax.numpy as jnp
from jax import lax
from jax.experimental import pallas as pl
from jax.experimental.pallas import tpu as pltpu
from jax.sharding import PartitionSpec as P

E = 128
MESH = pl.DeviceIdType.MESH
F32 = jnp.float32
BF16 = jnp.bfloat16
NT = (((1,), (1,)), ((), ()))
TN = (((0,), (0,)), ((), ()))
NN = (((1,), (0,)), ((), ()))
RATIO = 5
ROWS = 512
COLS = RATIO * E
WIDTH = 9 * E
MODEL = 5120
GROUP = 640
PIECE = 160
MASKED = -1e30
Z_STEPS = (2, 1, 3, 0)


def dot(a, b, dims):
    return lax.dot_general(a, b, dims, preferred_element_type=F32)


def stack_heads(ref, first):
    return jnp.concatenate(
        [ref[pl.ds(first, E), r * E : (r + 1) * E] for r in range(RATIO)], axis=0
    )


def kernel(
    q_hbm,
    k_hbm,
    v_hbm,
    lengths,
    w_hbm,
    gy_hbm,
    proj_hbm,
    dq_hbm,
    dk_hbm,
    dv_hbm,
    gw_hbm,
    proj_out,
    dq_out,
    dk_out,
    dv_out,
    gw_out,
    q,
    kw,
    vw,
    kv_relay,
    w,
    cot,
    att,
    up,
    up_acc,
    probs,
    scores,
    dk_acc,
    dv_acc,
    home_send,
    home_recv,
    part,
    core_recv,
    y_send,
    y_recv,
    stage,
    ax_recv,
    az_send,
    az_recv,
    bz_relay,
    bz_recv,
    bx_send,
    bx_recv,
    l_send,
    l_recv,
    local_sem,
    out_sem,
    kv_ss,
    kv_rs,
    kr_ss,
    kr_rs,
    kf_ss,
    own_ss,
    own_rs,
    ag_ss,
    ag_rs,
    fw_ss,
    fw_rs,
    home_ss,
    home_rs,
    hp_ss,
    hp_rs,
    pc_ss,
    pc_rs,
    py_ss,
    py_rs,
    ax_ss,
    ax_rs,
    az_ss,
    az_rs,
    br_ss,
    br_rs,
    bz_ss,
    bz_rs,
    bx_ss,
    bx_rs,
    l_ss,
    l_rs,
):
    c = lax.axis_index("ctx")
    h = lax.axis_index("head")
    z, yl, x = c // 8, (c // 4) % 2, c % 4
    core, yh = h % 2, h // 2
    h_core = h + 1 - 2 * core
    h_far = (h + 2) % 4
    core_dev = (c, h_core)
    far_dev = (c, h_far)
    lo_dev = (c + 4 - 8 * yl, h)

    def x_dev(step):
        return (c - x + (x + step) % 4, h)

    def z_dev(step):
        return ((c + 8 * step) % 32, h)

    def c_dev(step):
        return ((c + step + 32) % 32, h)

    sends = []

    def remote(src, dst, ss, rs, device):
        return pltpu.make_async_remote_copy(
            src_ref=src, dst_ref=dst, send_sem=ss, recv_sem=rs, device_id=device, device_id_type=MESH
        )

    def send(src, dst, ss, rs, device):
        copy = remote(src, dst, ss, rs, device)
        copy.start()
        sends.append(copy)
        return copy

    def rows_of(head):
        return pl.ds(pl.multiple_of(head * 128, 128), 128)

    own_rows = rows_of(h)
    far_rows = rows_of(h_far)

    def group_cols(n):
        first = (((z + Z_STEPS[n // 2]) % 4) * 2 + n % 2) * GROUP
        return pl.ds(pl.multiple_of(first, 128), GROUP)

    local = []
    for index, (src, dst) in enumerate(
        (
            (q_hbm, q),
            (k_hbm, kw.at[1024:1536]),
            (v_hbm, vw.at[1024:1536]),
            (gy_hbm, cot.at[own_rows]),
            (w_hbm, w),
        )
    ):
        copy = pltpu.make_async_copy(src, dst, local_sem.at[index])
        copy.start()
        local.append(copy)

    barrier = pltpu.get_barrier_semaphore()
    peers = [core_dev, far_dev, lo_dev]
    peers += [x_dev(s) for s in (1, 2, 3)] + [z_dev(s) for s in (1, 2, 3)]
    peers += [c_dev(s) for s in (1, 2, 3, 4, -1, -2, -3, -4)]
    for peer in peers:
        pl.semaphore_signal(barrier, inc=1, device_id=peer, device_id_type=MESH)
    pl.semaphore_wait(barrier, len(peers))

    near, far, relays, hops = [], [], [], []
    for index, (src, dst) in enumerate(((k_hbm, kw), (v_hbm, vw))):
        near_dst, far_dst, relay = dst.at[512:1024], dst.at[0:512], kv_relay.at[index]
        near_sem, far_sem = kv_rs.at[2 * index], kv_rs.at[2 * index + 1]
        near.append(remote(src, near_dst, kv_ss.at[2 * index], near_sem, c_dev(1)))
        far.append(remote(src, far_dst, kv_ss.at[2 * index + 1], far_sem, c_dev(2)))
        relays.append(remote(src, relay, kr_ss.at[index], kr_rs.at[index], c_dev(4)))
        hops.append(
            (
                remote(relay, near_dst, kf_ss.at[2 * index], near_sem, c_dev(-3)),
                remote(relay, far_dst, kf_ss.at[2 * index + 1], far_sem, c_dev(-2)),
            )
        )

    @pl.when(x >= 2)
    def _():
        relays[0].start()
        relays[1].start()

    for index in (0, 1):

        @pl.when(x != 3)
        def _():
            near[index].start()

        @pl.when(x < 2)
        def _():
            far[index].start()

    def pass_block(index):
        @pl.when(x >= 2)
        def _():
            relays[index].wait_recv()
            hops[index][1].start()

        @pl.when(x == 3)
        def _():
            hops[index][0].start()

    def receive_block(index):
        near[index].wait_recv()
        far[index].wait_recv()

    gathers = []
    for n in range(8):
        cols = group_cols(n)
        gathers.append(
            send(gy_hbm.at[:, cols], cot.at[own_rows, cols], ag_ss.at[n], ag_rs.at[n], far_dev)
        )
    own_copy = send(gy_hbm, cot.at[own_rows], own_ss.at[0], own_rs.at[0], core_dev)

    scale = E ** (-0.5)
    log2e = scale * math.log2(math.e)

    def mask_bias(tile, chunk):
        t = c * ROWS + tile * E + lax.broadcasted_iota(jnp.int32, (1, E), 1)
        start = jnp.zeros((1, E), jnp.int32)
        run = jnp.int32(0)
        for d in range(32):
            run = run + lengths[d]
            start = jnp.where(t >= run, run, start)
        return t, start

    def visible(t, start, tile, chunk):
        j = (c - 2) * ROWS + tile * E + chunk * E + lax.broadcasted_iota(jnp.int32, (E, E), 0)
        bias = jnp.where((j >= start) & (j <= t), 0.0, MASKED)
        return jnp.concatenate([bias] * RATIO, axis=1)

    local[0].wait()
    local[1].wait()
    pass_block(0)
    pass_block(1)
    receive_block(0)

    def weigh(tile, carry):
        first = pl.multiple_of(tile * E, E)
        t, start = mask_bias(tile, 0)
        qt = stack_heads(q, first)
        scores[...] = dot(kw[pl.ds(first, WIDTH), :], qt, NT)

        def largest(chunk, top):
            rows = pl.ds(pl.multiple_of(chunk * E, E), E)
            s = scores[rows, :] + visible(t, start, tile, chunk)
            scores[rows, :] = s
            return jnp.maximum(top, jnp.max(s.reshape(16, 8, COLS), axis=0))

        top = lax.fori_loop(0, 9, largest, jnp.full((8, COLS), MASKED, F32))
        top = jnp.max(top, axis=0, keepdims=True)

        def powers(chunk, total):
            rows = pl.ds(pl.multiple_of(chunk * E, E), E)
            p = jnp.exp2((scores[rows, :] - top) * log2e)
            scores[rows, :] = p
            return total + jnp.sum(p.reshape(16, 8, COLS), axis=0)

        total = lax.fori_loop(0, 9, powers, jnp.zeros((8, COLS), F32))
        inverse = 1.0 / jnp.sum(total, axis=0, keepdims=True)

        def normal(chunk, carry):
            rows = pl.ds(pl.multiple_of(chunk * E, E), E)
            probs[tile, rows, :] = (scores[rows, :] * inverse).astype(BF16)
            return carry

        lax.fori_loop(0, 9, normal, 0)
        return carry

    lax.fori_loop(0, 4, weigh, 0)
    local[2].wait()
    receive_block(1)

    def attend(tile, carry):
        first = pl.multiple_of(tile * E, E)
        out = dot(vw[pl.ds(first, WIDTH), :], probs[tile], TN)
        for r in range(RATIO):
            att[pl.ds(first, E), r * E : (r + 1) * E] = out[:, r * E : (r + 1) * E].T.astype(BF16)
        return carry

    lax.fori_loop(0, 4, attend, 0)

    forwards = []

    def forward(n):
        gathers[n].wait_recv()
        cols = group_cols(n)
        ref = cot.at[far_rows, cols]
        forwards.append(send(ref, ref, fw_ss.at[n], fw_rs.at[n], core_dev))

    ax, br, bz = {}, {}, {}

    def block_rows(step, first, count):
        return pl.ds(pl.multiple_of(((x + step) % 4) * PIECE + first, 16), count)

    def weight_group(n):
        forwards[n].wait_recv()
        step = Z_STEPS[n // 2]
        stage[n] = dot(cot[:, group_cols(n)], att[...], TN).astype(BF16)
        if n % 2 == 0:
            for dx in (2, 1, 3):
                slot = (n // 2) * 3 + dx - 1
                ax[n // 2, dx] = send(
                    stage.at[n, block_rows(dx, 0, PIECE)],
                    ax_recv.at[slot],
                    ax_ss.at[slot],
                    ax_rs.at[slot],
                    x_dev(dx),
                )
        elif step == 2:
            for dx in Z_STEPS:
                for way in (0, 1):
                    slot = 2 * dx + way
                    br[way, dx] = send(
                        stage.at[n, block_rows(dx, 80 * way, 80)],
                        bz_relay.at[slot],
                        br_ss.at[slot],
                        br_rs.at[slot],
                        z_dev((1, 3)[way]),
                    )

    def relay_z(way, dx):
        br[way, dx].wait_recv()
        rows = block_rows(dx, 80 * way, 80)
        slot = 2 * dx + way
        stage[2 * way + 3, rows, :] = (
            stage[2 * way + 3, rows, :].astype(F32) + bz_relay[slot].astype(F32)
        ).astype(BF16)
        whole = block_rows(dx, 0, PIECE)
        bz[way, dx] = send(
            stage.at[2 * way + 3, whole],
            bz_recv.at[way, whole],
            bz_ss.at[slot],
            bz_rs.at[slot],
            z_dev((1, 3)[way]),
        )

    def raise_up(pair):
        first = pl.multiple_of(((z + Z_STEPS[pair]) % 4) * 2 * GROUP, 128)
        columns = pl.ds(first, 2 * GROUP)
        more = dot(cot[:, columns], w[columns, :], NN)
        up_acc[...] = more if pair == 0 else up_acc[...] + more

    local[3].wait()
    own_copy.wait_recv()
    for n in range(4):
        forward(n)
    for n in range(4):
        weight_group(n)

    local[4].wait()

    def project(n, carry):
        first = pl.multiple_of(n * GROUP, 128)
        part[:, pl.ds(first, GROUP)] = dot(att[...], w[pl.ds(first, GROUP), :], NT).astype(BF16)
        return carry

    lax.fori_loop(0, 8, project, 0)
    to_core = {}
    for side in (1, 0):
        head = (h_core + 2 * side) % 4
        to_core[side] = send(
            part.at[rows_of(head)], core_recv.at[side], pc_ss.at[side], pc_rs.at[side], core_dev
        )
    for n in range(4, 6):
        forward(n)
    raise_up(0)
    raise_up(1)
    for dx in Z_STEPS:
        relay_z(0, dx)
    for n in (5, 4):
        weight_group(n)
    for dx in Z_STEPS:
        relay_z(1, dx)
    to_core[1].wait_recv()
    to_far = []

    def sum_core(n):
        cols = pl.ds(n * 1280, 1280)
        y_send[:, cols] = (part[far_rows, cols].astype(F32) + core_recv[1, :, cols].astype(F32)).astype(
            BF16
        )
        to_far.append(send(y_send.at[:, cols], y_recv.at[:, cols], py_ss.at[n], py_rs.at[n], far_dev))

    sum_core(0)
    raise_up(2)
    for n in range(6, 8):
        forward(n)
    for n in range(1, 4):
        sum_core(n)
    for n in range(6, 8):
        weight_group(n)
    raise_up(3)
    up[...] = up_acc[...].astype(BF16)

    az = {}

    def sum_x(index):
        step = Z_STEPS[index]
        total = stage[2 * index, block_rows(0, 0, PIECE), :].astype(F32)
        for dx in (1, 2, 3):
            ax[index, dx].wait_recv()
            total = total + ax_recv[index * 3 + dx - 1].astype(F32)
        if step:
            az_send[step - 1] = total.astype(BF16)
            az[step] = send(
                az_send.at[step - 1],
                az_recv.at[step - 1],
                az_ss.at[step - 1],
                az_rs.at[step - 1],
                z_dev(step),
            )
        return total

    bx = {}

    def sum_z(dx):
        rows = block_rows(dx, 0, PIECE)
        total = stage[7, rows, :].astype(F32)
        for way in (0, 1):
            bz[way, dx].wait_recv()
            total = total + bz_recv[way, rows, :].astype(F32)
        if dx:
            bx_send[dx - 1] = total.astype(BF16)
            bx[dx] = send(
                bx_send.at[dx - 1], bx_recv.at[dx - 1], bx_ss.at[dx - 1], bx_rs.at[dx - 1], x_dev(dx)
            )
        return total

    sum_x(0)

    dk_acc[...] = jnp.zeros_like(dk_acc)
    dv_acc[...] = jnp.zeros_like(dv_acc)

    def home_piece(index, tile):
        rows = pl.ds(pl.multiple_of(tile * E, E), E)
        slot = index * 2 + 1
        return remote(
            home_send.at[slot, rows],
            home_recv.at[slot, rows],
            hp_ss.at[index, tile],
            hp_rs.at[index, tile],
            c_dev(-2),
        )

    def backward(tile, carry):
        first = pl.multiple_of(tile * E, E)
        window = pl.ds(first, WIDTH)
        up_t = stack_heads(up, first)
        delta = []
        for r in range(RATIO):
            cols = slice(r * E, (r + 1) * E)
            prod = up[pl.ds(first, E), cols].astype(F32) * att[pl.ds(first, E), cols].astype(F32)
            delta.append(jnp.sum(prod.T, axis=0, keepdims=True))
        delta = jnp.concatenate(delta, axis=1)
        scores[...] = dot(vw[window, :], up_t, NT)
        dv_acc[window, :] += dot(probs[tile], up_t, NN)

        def grad(chunk, carry):
            rows = pl.ds(pl.multiple_of(chunk * E, E), E)
            weight = probs[tile, rows, :].astype(F32)
            probs[tile, rows, :] = (weight * (scores[rows, :] - delta)).astype(BF16)
            return carry

        lax.fori_loop(0, 9, grad, 0)
        dk_acc[window, :] += dot(probs[tile], stack_heads(q, first), NN)
        rows = pl.ds(first, E)
        home_send[1, rows] = (dk_acc[rows, :] * scale).astype(BF16)
        home_send[3, rows] = dv_acc[rows, :].astype(BF16)
        for index in (0, 1):
            home_piece(index, tile).start()
        dq = dot(kw[window, :], probs[tile], TN) * scale
        for r in range(RATIO):
            dq_out[pl.ds(first, E), r * E : (r + 1) * E] = dq[:, r * E : (r + 1) * E].T.astype(BF16)
        return carry

    lax.fori_loop(0, 1, backward, 0)
    sum_x(1)
    lax.fori_loop(1, 2, backward, 0)
    sum_z(2)
    lax.fori_loop(2, 3, backward, 0)
    sum_z(1)
    sum_x(2)
    lax.fori_loop(3, 4, backward, 0)
    sum_z(3)
    total_a = sum_x(3)
    total_b = sum_z(0)
    homes = [home_piece(index, tile) for index in (0, 1) for tile in range(4)]
    sends.extend(homes)
    for index, acc in enumerate((dk_acc, dv_acc)):
        factor = scale if index == 0 else 1.0
        slot = index * 2
        home_send[slot] = (acc[512:1024, :] * factor).astype(BF16)
        homes.append(
            send(
                home_send.at[slot],
                home_recv.at[slot],
                home_ss.at[index],
                home_rs.at[index],
                c_dev(-1),
            )
        )

    outs = []

    def write(index, src, dst):
        copy = pltpu.make_async_copy(src, dst, out_sem.at[index])
        copy.start()
        outs.append(copy)

    write(0, dq_out, dq_hbm)
    for dz in (1, 2, 3):
        az[dz].wait_recv()
        total_a = total_a + az_recv[dz - 1].astype(F32)
    for dx in (1, 2, 3):
        bx[dx].wait_recv()
        total_b = total_b + bx_recv[dx - 1].astype(F32)
    lower = yl == 0
    l_send[...] = jnp.where(lower, total_b, total_a).astype(BF16)
    last = send(l_send, l_recv, l_ss.at[0], l_rs.at[0], lo_dev)

    for copy in homes:
        copy.wait_recv()
    for index, (acc, out) in enumerate(((dk_acc, dk_out), (dv_acc, dv_out))):
        factor = scale if index == 0 else 1.0
        total = acc[1024:1536, :] * factor
        for step in (1, 2):
            total = total + home_recv[index * 2 + step - 1].astype(F32)
        out[...] = total.astype(BF16)
        write(1 + index, out, (dk_hbm, dv_hbm)[index])

    to_core[0].wait_recv()
    for n in range(4):
        cols = pl.ds(n * 1280, 1280)
        to_far[n].wait_recv()
        proj_out[:, cols] = (
            part[own_rows, cols].astype(F32)
            + core_recv[0, :, cols].astype(F32)
            + y_recv[:, cols].astype(F32)
        ).astype(BF16)
        write(3 + n, proj_out.at[:, cols], proj_hbm.at[:, cols])

    last.wait_recv()
    mine = jnp.where(lower, total_a, total_b)
    gw_out[...] = (mine + l_recv[...].astype(F32)) * (1.0 / 128.0)
    write(7, gw_out, gw_hbm)
    for copy in sends:
        copy.wait_send()
    for index in (0, 1):

        @pl.when(x != 3)
        def _():
            near[index].wait_send()

        @pl.when(x < 2)
        def _():
            far[index].wait_send()

        @pl.when(x >= 2)
        def _():
            relays[index].wait_send()
            hops[index][1].wait_send()

        @pl.when(x == 3)
        def _():
            hops[index][0].wait_send()

    for copy in outs:
        copy.wait()


def keep(*refs):
    for src, dst in zip(refs[:5], refs[5:]):
        dst[...] = src[...]


def on_device(queries, keys, values, lengths, w_out, grad_y):
    hbm = pl.BlockSpec(memory_space=pl.ANY)
    vmem = pl.BlockSpec(memory_space=pltpu.VMEM)
    dma = lambda *n: pltpu.SemaphoreType.DMA(n)
    shapes = (
            jax.ShapeDtypeStruct((128, MODEL), BF16),
            jax.ShapeDtypeStruct((ROWS, COLS), BF16),
            jax.ShapeDtypeStruct((ROWS, E), BF16),
            jax.ShapeDtypeStruct((ROWS, E), BF16),
            jax.ShapeDtypeStruct((PIECE, COLS), F32),
    )
    results = pl.pallas_call(
        kernel,
        out_shape=shapes,
        in_specs=[hbm, hbm, hbm, pl.BlockSpec(memory_space=pltpu.SMEM), hbm, hbm],
        out_specs=(hbm,) * 5,
        scratch_shapes=[
            *[pltpu.VMEM(s.shape, s.dtype) for s in shapes],
            pltpu.VMEM((ROWS, COLS), BF16),
            pltpu.VMEM((3 * ROWS, E), BF16),
            pltpu.VMEM((3 * ROWS, E), BF16),
            pltpu.VMEM((2, ROWS, E), BF16),
            pltpu.VMEM((MODEL, COLS), BF16),
            pltpu.VMEM((ROWS, MODEL), BF16),
            pltpu.VMEM((ROWS, COLS), BF16),
            pltpu.VMEM((ROWS, COLS), BF16),
            pltpu.VMEM((ROWS, COLS), F32),
            pltpu.VMEM((4, WIDTH, COLS), BF16),
            pltpu.VMEM((WIDTH, COLS), F32),
            pltpu.VMEM((3 * ROWS, E), F32),
            pltpu.VMEM((3 * ROWS, E), F32),
            pltpu.VMEM((4, ROWS, E), BF16),
            pltpu.VMEM((4, ROWS, E), BF16),
            pltpu.VMEM((ROWS, MODEL), BF16),
            pltpu.VMEM((2, 128, MODEL), BF16),
            pltpu.VMEM((128, MODEL), BF16),
            pltpu.VMEM((128, MODEL), BF16),
            pltpu.VMEM((8, GROUP, COLS), BF16),
            pltpu.VMEM((12, PIECE, COLS), BF16),
            pltpu.VMEM((3, PIECE, COLS), BF16),
            pltpu.VMEM((3, PIECE, COLS), BF16),
            pltpu.VMEM((8, 80, COLS), BF16),
            pltpu.VMEM((2, GROUP, COLS), BF16),
            pltpu.VMEM((3, PIECE, COLS), BF16),
            pltpu.VMEM((3, PIECE, COLS), BF16),
            pltpu.VMEM((PIECE, COLS), BF16),
            pltpu.VMEM((PIECE, COLS), BF16),
            dma(5),
            dma(8),
            dma(4),
            dma(4),
            dma(2),
            dma(2),
            dma(4),
            dma(1),
            dma(1),
            dma(8),
            dma(8),
            dma(8),
            dma(8),
            dma(2),
            dma(2),
            dma(2, 4),
            dma(2, 4),
            dma(2),
            dma(2),
            dma(4),
            dma(4),
            dma(12),
            dma(12),
            dma(3),
            dma(3),
            dma(8),
            dma(8),
            dma(8),
            dma(8),
            dma(3),
            dma(3),
            dma(1),
            dma(1),
        ],
        compiler_params=pltpu.CompilerParams(
            collective_id=0, has_side_effects=True, vmem_limit_bytes=63 << 20
        ),
    )(queries, keys, values, lengths, w_out, grad_y)
    halves = tuple(pl.BlockSpec((s.shape[0] // 2, s.shape[1]), lambda i: (i, 0)) for s in shapes)
    return pl.pallas_call(
        keep, grid=(2,), out_shape=shapes, in_specs=list(halves), out_specs=halves
    )(*results)


def solution(mesh):
    in_specs = (
        P("ctx", "head"),
        P("ctx", "head"),
        P("ctx", "head"),
        P(),
        P(None, "head"),
        P(("ctx", "head"), None),
    )
    out_specs = (
        P(("ctx", "head"), None),
        P("ctx", "head"),
        P("ctx", "head"),
        P("ctx", "head"),
        P("ctx", "head"),
    )
    return jax.shard_map(
        on_device, mesh=mesh, in_specs=in_specs, out_specs=out_specs, check_vma=False
    )
```
